32 devices in a mesh: node: 8 (over z, core), local: 4 (over y, x).
Axes of the slice: x: 2, y: 2, z: 4, core: 2. Of those that a mesh axis runs over, the one named last changes fastest.
Arguments:
- tokens: bfloat16 [4096, 8192], P(('node', 'local')), may hold values from -6 to 6
- upstream: bfloat16 [4096, 8192], P(('node', 'local')), may hold values from -1.5 to 1.5
- router_probs: float32 [4096, 64], P(('node', 'local')), may hold values from 0.01 to 0.3
- expert_ids: int32 [4096, 2], P(('node', 'local')), may hold values from 0 to 63, as said below
- slot_index: int32 [4096, 2], P(('node', 'local')), may hold values from -1 to 3, as said below
- w_in: bfloat16 [2, 8192, 16384], P(None, 'local', 'node'), may hold values from -0.0625 to 0.0625
- w_out: bfloat16 [2, 16384, 8192], P(None, 'node', 'local'), may hold values from -0.046875 to 0.046875
- router_weight: bfloat16 [8192, 64], replicated, may hold values from -0.125 to 0.125
Outputs:
- token_grads: bfloat16 [4096, 8192], P(('node', 'local'))
- w_in_grad: bfloat16 [2, 8192, 16384], P(None, 'local', 'node')
- w_out_grad: bfloat16 [2, 16384, 8192], P(None, 'node', 'local')
- router_grad: float32 [8192, 64], P(('node', 'local'))
The draws below stay inside these ranges and needn't reach their ends.
Inputs may be any that keep to these rules, and one draw needn't show every extreme that they name: `expert_ids`: each token names two different experts. `slot_index`: an assignment to an expert under 2 has as slot its rank among its device's 128 tokens' assignments to that expert, in an order drawn at random, and -1 when that rank is 4 or more; every assignment to another expert has -1. In every draw some expert under 2 fills all 4 slots from every device.
All inputs are finite; a program needn't handle non-finite values.
Results may differ from the reference program's by a relative error of at most 0.017.
Values may be sent and summed in bfloat16 or wider, within the bound.
A program may use at most 128 MiB of HBM per device.

```python
import math
import jax
import jax.numpy as jnp
from jax import lax

D = 8192
FF = 16384
EXP_ALL = 64
FLIGHT = 2
TOK_DEV = 128
CAP = 4
TOKENS = 4096


def routing_tables(key):
    keys = jax.random.split(key, 6)
    blocks = TOKENS // TOK_DEV
    first_pick = jax.random.randint(keys[0], (TOKENS,), 0, EXP_ALL, dtype=jnp.int32)
    offset_one = jax.random.randint(keys[1], (TOKENS,), 1, EXP_ALL, dtype=jnp.int32)
    second_pick = (first_pick + offset_one) % EXP_ALL
    hot_expert = jax.random.randint(keys[2], (), 0, FLIGHT, dtype=jnp.int32)
    block_keys = jax.random.split(keys[3], blocks)
    order = jax.vmap(lambda subkey: jax.random.permutation(subkey, TOK_DEV).astype(jnp.int32))(block_keys).reshape(TOKENS)
    chosen = order < CAP
    offset_two = jax.random.randint(keys[4], (TOKENS,), 1, EXP_ALL, dtype=jnp.int32)
    first_pick = jnp.where(chosen, hot_expert, first_pick)
    clash = jnp.logical_and(chosen, second_pick == hot_expert)
    second_pick = jnp.where(clash, (hot_expert + offset_two) % EXP_ALL, second_pick)
    ids_table = jnp.stack([first_pick, second_pick], axis=1).astype(jnp.int32)
    rank_keys = jax.random.split(keys[5], blocks)
    priority = jax.vmap(lambda subkey: jax.random.permutation(subkey, 2 * TOK_DEV).astype(jnp.int32))(rank_keys)
    block_ids = ids_table.reshape(blocks, 2 * TOK_DEV)

    def ranking(ids_row, prio_row):
        same_expert = ids_row[:, None] == ids_row[None, :]
        ahead = prio_row[None, :] < prio_row[:, None]
        return jnp.sum(jnp.logical_and(same_expert, ahead).astype(jnp.int32), axis=1).astype(jnp.int32)
    ranks = jax.vmap(ranking)(block_ids, priority).reshape(TOKENS, 2)
    held = jnp.logical_and(ranks < CAP, ids_table < FLIGHT)
    slot_table = jnp.where(held, ranks, -1).astype(jnp.int32)
    return (ids_table, slot_table)


def draw_expert_ids(key, part):
    return routing_tables(key)[0]


def draw_slot_index(key, part):
    return routing_tables(key)[1]


def spiked(entries, stream_key, source, target, shards_of, factor):
    def block_of(dim):
        return (jnp.arange(entries.shape[dim]) // (entries.shape[dim] // shards_of)).reshape((-1,) + (1,) * (entries.ndim - 1 - dim))

    near = jax.random.permutation(stream_key, shards_of)[block_of(target)]
    far = (block_of(target) + shards_of // 2) % shards_of
    return jnp.where((block_of(source) == near) | (block_of(source) == far), factor * entries, entries)


def block_scale(stream_key, dims, pieces, least, high):
    def one(axis_at, parts):
        steps = jax.random.uniform(jax.random.fold_in(jax.random.fold_in(stream_key, 6), axis_at), (parts,), jnp.float32, least / len(pieces), high / len(pieces))
        return jnp.repeat(jnp.exp(steps), dims[axis_at] // parts).reshape((-1,) + (1,) * (len(dims) - axis_at - 1))

    gain = one(*pieces[0])
    for cut in pieces[1:]:
        gain = gain * one(*cut)
    return gain


def scatter_about(own_key, shape, scale, bound, cuts=(), held_as=jnp.bfloat16):
    array = jax.random.normal(own_key, shape, jnp.float32) * scale
    if len(cuts) > 0:
        array = block_scale(own_key, shape, cuts, -0.22, 0.18) * array
    return jnp.clip(array, min=-bound, max=bound).astype(held_as)


def bell_draw_with(stream_key, extent, spread, limit, cuts, heavy, kind=jnp.bfloat16):
    result = spread * jax.random.normal(stream_key, extent, jnp.float32)
    if cuts:
        result = result * block_scale(stream_key, extent, cuts, -0.22, 0.18)
    return jnp.clip(spiked(result, jax.random.fold_in(stream_key, 3), *heavy), -limit, limit).astype(kind)


def setup_inputs(seed: int = 0) -> dict:
    arg_keys = jax.random.split(jax.random.key(seed), 9)
    tokens = bell_draw_with(arg_keys[0], (TOKENS, D), 1.0, 6.0, ((0, 32),), (0, 1, 32, 2.75))
    upstream = scatter_about(arg_keys[1], (TOKENS, D), 0.25, 1.5, ((0, 32),))
    router_probs = jnp.clip(jnp.exp(math.log(0.3) - 3.4011974 * jax.random.uniform(arg_keys[2], (TOKENS, EXP_ALL), jnp.float32) ** block_scale(arg_keys[2], (TOKENS, EXP_ALL), ((0, 32),), -0.2, 0.2)), 0.01, 0.3)
    expert_ids = draw_expert_ids(jax.random.fold_in(arg_keys[8], 71), 0)
    slot_index = draw_slot_index(jax.random.fold_in(arg_keys[8], 71), 0)
    w_in = scatter_about(arg_keys[5], (FLIGHT, D, FF), D ** -0.5, 0.0625, ((1, 4), (2, 8)))
    w_out = scatter_about(arg_keys[6], (FLIGHT, FF, D), FF ** -0.5, 0.046875, ((1, 8), (2, 4)))
    router_weight = scatter_about(arg_keys[7], (D, EXP_ALL), (D // 4) ** -0.5, 0.125)
    return {"tokens": tokens, "upstream": upstream, "router_probs": router_probs, "expert_ids": expert_ids, "slot_index": slot_index, "w_in": w_in, "w_out": w_out, "router_weight": router_weight}


root_two_pi = math.sqrt(2.0 / math.pi)
cubic_coef = 0.044715

def gelu_pair(pre):
    inner = root_two_pi * (pre + cubic_coef * pre * pre * pre)
    tangent = jnp.tanh(inner)
    value = 0.5 * pre * (1.0 + tangent)
    slope = 0.5 * (1.0 + tangent) + 0.5 * pre * (1.0 - tangent * tangent) * root_two_pi * (1.0 + 3.0 * cubic_coef * pre * pre)
    return (value, slope)

def reference(tokens, upstream, router_probs, expert_ids, slot_index, w_in, w_out, router_weight):
    span = TOKENS // TOK_DEV * CAP
    owner = (jnp.arange(TOKENS, dtype=jnp.int32) // TOK_DEV).astype(jnp.int32)[:, None]
    is_kept = slot_index >= 0
    safe_expert = jnp.where(is_kept, expert_ids, 0).astype(jnp.int32)
    position = (owner * CAP + jnp.where(is_kept, slot_index, 0)).astype(jnp.int32)
    flat_place = jnp.where(is_kept, safe_expert * span + position, FLIGHT * span).astype(jnp.int32)
    token_numbers = jnp.broadcast_to(jnp.arange(TOKENS, dtype=jnp.int32)[:, None], (TOKENS, 2))
    token_of = jnp.full((FLIGHT * span,), -1, jnp.int32).at[flat_place.reshape(-1)].set(token_numbers.reshape(-1), mode='drop').reshape(FLIGHT, span)

    def expert(packed):
        expert_number, first_matrix, second_matrix, row_tokens = packed
        valid = row_tokens >= 0
        safe_rows = jnp.where(valid, row_tokens, 0).astype(jnp.int32)
        rows_in = jnp.where(valid[:, None], tokens[safe_rows], jnp.zeros((), tokens.dtype))
        rows_up = jnp.where(valid[:, None], upstream[safe_rows], jnp.zeros((), upstream.dtype))
        gate_rows = jnp.where(valid, router_probs[safe_rows, expert_number], jnp.zeros((), jnp.float32)).astype(jnp.bfloat16)
        gate_wide = gate_rows.astype(jnp.float32)[:, None]
        pre = jnp.dot(rows_in, first_matrix, preferred_element_type=jnp.float32)
        value, slope = gelu_pair(pre)
        act = value.astype(jnp.bfloat16)
        upw = jnp.dot(rows_up, second_matrix.T, preferred_element_type=jnp.float32)
        scores = lax.optimization_barrier(jnp.sum(act.astype(jnp.float32) * upw, axis=1))
        pre_grad = (gate_wide * upw * slope).astype(jnp.bfloat16)
        out_grad = (gate_wide * rows_up.astype(jnp.float32)).astype(jnp.bfloat16)
        second_grad = jnp.dot(act.T, out_grad, preferred_element_type=jnp.float32).astype(jnp.bfloat16)
        first_grad = jnp.dot(rows_in.T, pre_grad, preferred_element_type=jnp.float32).astype(jnp.bfloat16)
        row_grads = jnp.dot(pre_grad, first_matrix.T, preferred_element_type=jnp.float32).astype(jnp.bfloat16)
        return (first_grad, second_grad, row_grads, scores)
    w_in_grad, w_out_grad, row_grads, scores = lax.map(expert, (jnp.arange(FLIGHT, dtype=jnp.int32), w_in, w_out, token_of))
    combined = jnp.zeros((TOKENS, D), jnp.float32)
    for which in range(2):
        picked = row_grads[safe_expert[:, which], position[:, which]].astype(jnp.float32)
        combined = combined + jnp.where(is_kept[:, which, None], picked, jnp.zeros((), jnp.float32))
    gate_grad = jnp.where(is_kept, scores[safe_expert, position], jnp.zeros((), jnp.float32))
    expert_iota = jnp.arange(EXP_ALL, dtype=jnp.int32)
    matches = expert_ids[:, :, None] == expert_iota[None, None, :]
    prob_grad = lax.optimization_barrier(jnp.sum(jnp.where(matches, gate_grad[:, :, None], jnp.zeros((), jnp.float32)), axis=1))
    centred = prob_grad - lax.optimization_barrier(jnp.sum(router_probs * prob_grad, axis=1, keepdims=True))
    logit_grad = (router_probs * centred).astype(jnp.bfloat16)
    router_grad = jnp.dot(tokens.T, logit_grad, preferred_element_type=jnp.float32)
    router_part = jnp.dot(logit_grad, router_weight.T, preferred_element_type=jnp.float32)
    token_grads = (combined + router_part).astype(jnp.bfloat16)
    return (token_grads, w_in_grad, w_out_grad, router_grad)
```

```python
import math

import jax
import jax.numpy as jnp
from jax import lax
from jax.experimental import pallas as pl
from jax.experimental.pallas import tpu as pltpu
from jax.sharding import PartitionSpec as P

CAP = 4
PAD = 128
MESH = pl.DeviceIdType.MESH
VMEM_BYTES = 60 * 1024 * 1024


root_two_pi = math.sqrt(2.0 / math.pi)
cubic_coef = 0.044715


def gelu_pair(pre):
    inner = root_two_pi * (pre + cubic_coef * pre * pre * pre)
    tangent = jnp.tanh(inner)
    value = 0.5 * pre * (1.0 + tangent)
    slope = 0.5 * (1.0 + tangent) + 0.5 * pre * (1.0 - tangent * tangent) * root_two_pi * (
        1.0 + 3.0 * cubic_coef * pre * pre
    )
    return (value, slope)


def contract(left, right, left_dim, right_dim):
    return lax.dot_general(
        left, right, (((left_dim,), (right_dim,)), ((), ())), preferred_element_type=jnp.float32
    )


def one_hot_rows(out_rows, in_rows, source):
    at = lax.broadcasted_iota(jnp.int32, (out_rows, in_rows), 0)
    column = lax.broadcasted_iota(jnp.int32, (out_rows, in_rows), 1)
    return (source(at) == column).astype(jnp.bfloat16)


def gate_column(blocks, expert):
    flat = blocks.reshape(-1, PAD).astype(jnp.float32)
    lane = lax.broadcasted_iota(jnp.int32, flat.shape, 1)
    return jnp.sum(jnp.where(lane == expert, flat, 0.0), axis=1, keepdims=True)


def exchange(dims, send, w_in, w_out, rows_out, hidden_out, scores_out, home_out,
             w_in_v, w_out_v, first, rows_v, part_s, part_r, own, hidden_v, terms, terms_r,
             core_sum, node_r, grads, home_s, home_r, score_1, score_2, score_3,
             w_sem, out_sem, a_s, a_r, z_s, z_r, c_s, c_r, p_s, p_r, g_s, g_r, t_s, t_r,
             n_s, n_r, h_s, h_r, s1_s, s1_r, s2_s, s2_r, s3_s, s3_r):
    nodes, locals_, flight, width, hidden = dims
    chips = nodes // 2
    span = locals_ * CAP
    rows = nodes * span
    piece = hidden // locals_
    node = lax.axis_index("node")
    loc = lax.axis_index("local")
    core = lax.rem(node, 2)
    chip = node // 2

    def local_peer(d):
        return (node, lax.rem(loc + d, locals_))

    def chip_peer(d):
        return (lax.rem(chip + d, chips) * 2 + core, loc)

    sibling = (chip * 2 + 1 - core, loc)
    peers = [local_peer(d) for d in range(1, locals_)]
    peers += [chip_peer(d) for d in range(1, chips)] + [sibling]

    def remote(src, dst, send_sem, recv_sem, peer):
        return pltpu.make_async_remote_copy(
            src_ref=src, dst_ref=dst, send_sem=send_sem, recv_sem=recv_sem,
            device_id=peer, device_id_type=MESH,
        )

    loads = []
    for e in range(flight):
        loads.append(pltpu.make_async_copy(w_in.at[e], w_in_v.at[e], w_sem.at[2 * e]))
        loads.append(pltpu.make_async_copy(w_out.at[e], w_out_v.at[e], w_sem.at[2 * e + 1]))
    for load in loads:
        load.start()

    barrier = pltpu.get_barrier_semaphore()
    for peer in peers:
        pl.semaphore_signal(barrier, inc=1, device_id=peer, device_id_type=MESH)
    pl.semaphore_wait(barrier, len(peers))

    sent = []

    def launch(copies):
        for copy in copies:
            copy.start()
        sent.extend(copies)
        return copies

    def arrive(copies):
        for copy in copies:
            copy.wait_recv()

    moved = launch([
        remote(send.at[lax.rem(loc + d, locals_)], first.at[loc], a_s.at[d], a_r.at[d], local_peer(d))
        for d in range(1, locals_)
    ])
    first[loc] = send[loc]
    arrive(moved)
    kinds = 2 * flight
    block = kinds * CAP

    def gather_source(i):
        k, rest = i // span, lax.rem(i, span)
        return (rest // CAP) * block + k * CAP + lax.rem(rest, CAP)

    order = one_hot_rows(kinds * span, locals_ * block, gather_source)
    ordered = contract(order, first[...].reshape(locals_ * block, width + PAD), 1, 0)
    ordered = ordered.astype(jnp.bfloat16)
    for e in range(flight):
        rows_v[e, node] = ordered[e * 2 * span:(e + 1) * 2 * span]

    def to_chips(e):
        copies = launch([
            remote(rows_v.at[e, node], rows_v.at[e, node], z_s.at[e, d], z_r.at[e, d], chip_peer(d))
            for d in range(1, chips)
        ])
        return copies, launch([
            remote(rows_v.at[e, node], rows_v.at[e, node], c_s.at[e, 0], c_r.at[e, 0], sibling)
        ])

    def finish_rows(e, copies, over):
        for d in range(1, chips):
            copies[d - 1].wait_recv()
            at = lax.rem(chip + chips - d, chips) * 2 + core
            over = over + launch([
                remote(rows_v.at[e, at], rows_v.at[e, at], c_s.at[e, d], c_r.at[e, d], sibling)
            ])
        return over

    def project(e):
        loads[2 * e].wait()
        loads[2 * e + 1].wait()
        left = rows_v[e, :, 0:span, 0:width].reshape(rows, width)
        up = rows_v[e, :, span:2 * span, 0:width].reshape(rows, width)
        copies = []
        tile = min(piece, 256)
        for d in list(range(1, locals_)) + [0]:
            base = lax.rem(loc + d, locals_) * piece

            def column(j, carry):
                at = pl.ds(pl.multiple_of(base + j * tile, tile), tile)
                to = pl.ds(pl.multiple_of(j * tile, tile), tile)
                pre = contract(left, w_in_v[e, :, at], 1, 0)
                upw = contract(up, w_out_v[e, at, :], 1, 1)
                if d == 0:
                    own[0, :, to] = pre
                    own[1, :, to] = upw
                else:
                    part_s[e, d - 1, 0, :, to] = pre.astype(jnp.bfloat16)
                    part_s[e, d - 1, 1, :, to] = upw.astype(jnp.bfloat16)
                return carry

            lax.fori_loop(0, piece // tile, column, 0)
            if d > 0:
                copies += launch([
                    remote(part_s.at[e, d - 1], part_r.at[e, d - 1], p_s.at[e, d], p_r.at[e, d],
                           local_peer(d))
                ])
        return copies

    def hidden_step(e, copies):
        arrive(copies)
        gate = gate_column(rows_v[e, :, 0:span, width:width + PAD], e)
        pre, upw = own[0], own[1]
        for d in range(locals_ - 1):
            pre = pre + part_r[e, d, 0].astype(jnp.float32)
            upw = upw + part_r[e, d, 1].astype(jnp.float32)
        value, slope = gelu_pair(pre)
        act = value.astype(jnp.bfloat16)
        here = pl.ds(pl.multiple_of(loc * piece, piece), piece)
        hidden_v[e, 0, :, here] = act
        hidden_v[e, 1, :, here] = (gate * upw * slope).astype(jnp.bfloat16)
        score_1[loc, 8 * e:8 * e + 8] = lax.dot_general(
            jnp.ones((8, piece), jnp.float32), act.astype(jnp.float32) * upw,
            (((1,), (1,)), ((), ())), precision=lax.Precision.HIGHEST,
            preferred_element_type=jnp.float32,
        )
        mine = hidden_v.at[e, :, :, here]
        return launch([
            remote(mine, mine, g_s.at[e, d], g_r.at[e, d], local_peer(d)) for d in range(1, locals_)
        ])

    def row_terms(e, copies):
        arrive(copies)
        tile = min(width, 512)

        def column(j, carry):
            at = pl.ds(pl.multiple_of(j * tile, tile), tile)
            made = contract(hidden_v[e, 1], w_in_v[e, at, :], 1, 1).astype(jnp.bfloat16)
            terms[e, :, :, :, at] = made.reshape(chips, 2, span, tile)
            return carry

        lax.fori_loop(0, width // tile, column, 0)
        return launch([
            remote(terms.at[e, :, 1 - core], terms_r.at[e], t_s.at[e], t_r.at[e], sibling)
        ])

    def reduce_nodes(e, copies):
        arrive(copies)
        core_sum[e] = (
            terms[e, :, core].astype(jnp.float32) + terms_r[e].astype(jnp.float32)
        ).astype(jnp.bfloat16)
        return launch([
            remote(core_sum.at[e, lax.rem(chip + d, chips)], node_r.at[e, d - 1], n_s.at[e, d],
                   n_r.at[e, d], chip_peer(d))
            for d in range(1, chips)
        ])

    def finish_grads(e, copies):
        arrive(copies)
        total = core_sum[e, chip].astype(jnp.float32)
        for d in range(chips - 1):
            total = total + node_r[e, d].astype(jnp.float32)
        grads[e] = total.astype(jnp.bfloat16)

    z_0, over_0 = to_chips(0)
    over_0 = finish_rows(0, z_0, over_0)
    z_1, over_1 = to_chips(1)
    arrive(over_0)
    parts_0 = project(0)
    over_1 = finish_rows(1, z_1, over_1)
    hidden_0 = hidden_step(0, parts_0)
    arrive(over_1)
    rows_copy = pltpu.make_async_copy(rows_v, rows_out, out_sem.at[0])
    rows_copy.start()
    parts_1 = project(1)
    terms_0 = row_terms(0, hidden_0)
    hidden_1 = hidden_step(1, parts_1)

    near = launch([
        remote(score_1.at[loc], score_1.at[loc], s1_s.at[d], s1_r.at[d], local_peer(d))
        for d in range(1, locals_)
    ])
    nodes_0 = reduce_nodes(0, terms_0)
    arrive(near)
    score_2[chip] = jnp.sum(score_1[...], axis=0)
    along = launch([
        remote(score_2.at[chip], score_2.at[chip], s2_s.at[d], s2_r.at[d], chip_peer(d))
        for d in range(1, chips)
    ])
    terms_1 = row_terms(1, hidden_1)
    hidden_copy = pltpu.make_async_copy(hidden_v, hidden_out, out_sem.at[1])
    hidden_copy.start()
    arrive(along)
    score_3[core] = jnp.sum(score_2[...], axis=0)
    across = launch([
        remote(score_3.at[core], score_3.at[core], s3_s.at[0], s3_r.at[0], sibling)
    ])
    nodes_1 = reduce_nodes(1, terms_1)
    finish_grads(0, nodes_0)
    arrive(across)
    scores_out[...] = score_3[0] + score_3[1]
    finish_grads(1, nodes_1)

    def home_source(i):
        at, rest = i // (flight * CAP), lax.rem(i, flight * CAP)
        return (rest // CAP) * span + at * CAP + lax.rem(rest, CAP)

    pick = one_hot_rows(locals_ * flight * CAP, flight * span, home_source)
    picked = contract(pick, grads[...].reshape(flight * span, width), 1, 0)
    home_s[...] = picked.reshape(locals_, flight * CAP, width)
    home = launch([
        remote(home_s.at[lax.rem(loc + d, locals_)], home_r.at[loc], h_s.at[d], h_r.at[d],
               local_peer(d))
        for d in range(1, locals_)
    ])
    home_r[loc] = home_s[loc]
    arrive(home)
    home_out[...] = home_r[...]
    for copy in sent:
        copy.wait_send()
    rows_copy.wait()
    hidden_copy.wait()


def run_exchange(send, w_in, w_out, nodes, locals_):
    flight, width, hidden = w_in.shape
    chips = nodes // 2
    span = locals_ * CAP
    rows = nodes * span
    piece = hidden // locals_
    wide = width + PAD
    block = send.shape[1]
    half, full = jnp.bfloat16, jnp.float32
    dma = pltpu.SemaphoreType.DMA
    vmem = pl.BlockSpec(memory_space=pltpu.VMEM)
    hbm = pl.BlockSpec(memory_space=pl.ANY)

    def kernel(*refs):
        exchange((nodes, locals_, flight, width, hidden), *refs)

    return pl.pallas_call(
        kernel,
        out_shape=(
            jax.ShapeDtypeStruct((flight, nodes, 2 * span, wide), half),
            jax.ShapeDtypeStruct((flight, 2, rows, hidden), half),
            jax.ShapeDtypeStruct((flight * 8, rows), full),
            jax.ShapeDtypeStruct((locals_, flight * CAP, width), full),
        ),
        in_specs=[vmem, hbm, hbm],
        out_specs=(hbm, hbm, vmem, vmem),
        scratch_shapes=[
            pltpu.VMEM((flight, width, hidden), half),
            pltpu.VMEM((flight, hidden, width), half),
            pltpu.VMEM((locals_, block, wide), half),
            pltpu.VMEM((flight, nodes, 2 * span, wide), half),
            pltpu.VMEM((flight, locals_ - 1, 2, rows, piece), half),
            pltpu.VMEM((flight, locals_ - 1, 2, rows, piece), half),
            pltpu.VMEM((2, rows, piece), full),
            pltpu.VMEM((flight, 2, rows, hidden), half),
            pltpu.VMEM((flight, chips, 2, span, width), half),
            pltpu.VMEM((flight, chips, span, width), half),
            pltpu.VMEM((flight, chips, span, width), half),
            pltpu.VMEM((flight, chips - 1, span, width), half),
            pltpu.VMEM((flight, span, width), half),
            pltpu.VMEM((locals_, flight * CAP, width), full),
            pltpu.VMEM((locals_, flight * CAP, width), full),
            pltpu.VMEM((locals_, flight * 8, rows), full),
            pltpu.VMEM((chips, flight * 8, rows), full),
            pltpu.VMEM((2, flight * 8, rows), full),
            dma((2 * flight,)), dma((2,)),
            dma((locals_,)), dma((locals_,)),
            dma((flight, chips)), dma((flight, chips)),
            dma((flight, chips)), dma((flight, chips)),
            dma((flight, locals_)), dma((flight, locals_)),
            dma((flight, locals_)), dma((flight, locals_)),
            dma((flight,)), dma((flight,)),
            dma((flight, chips)), dma((flight, chips)),
            dma((locals_,)), dma((locals_,)),
            dma((locals_,)), dma((locals_,)),
            dma((chips,)), dma((chips,)),
            dma((1,)), dma((1,)),
        ],
        compiler_params=pltpu.CompilerParams(
            collective_id=0, has_side_effects=True, vmem_limit_bytes=VMEM_BYTES
        ),
        cost_estimate=pl.CostEstimate(
            flops=6 * flight * rows * width * hidden,
            bytes_accessed=4 * flight * width * hidden,
            transcendentals=flight * rows * piece,
        ),
        name="exchange",
    )(send, w_in, w_out)


def weight_grads(rows_all, hidden_all, width):
    flight, nodes, double, wide = rows_all.shape
    span = double // 2
    rows, hidden = hidden_all.shape[2:]
    steps = 8
    high, low = hidden // steps, width // steps

    def kernel(rows_ref, act_ref, grad_ref, left_ref, out_ref, in_ref, out_grad):
        e, step = pl.program_id(0), pl.program_id(1)

        @pl.when(step == 0)
        def _():
            gate = gate_column(rows_ref[0, :, 0:span, width:wide], e)
            up = rows_ref[0, :, span:double, 0:width].reshape(rows, width)
            out_grad[...] = (gate * up.astype(jnp.float32)).astype(jnp.bfloat16)

        out_ref[0] = contract(act_ref[0, 0], out_grad[...], 0, 0).astype(jnp.bfloat16)
        left = left_ref[0, :, 0:span].reshape(rows, low)
        in_ref[0] = contract(left, grad_ref[0, 0], 0, 0).astype(jnp.bfloat16)

    return pl.pallas_call(
        kernel,
        grid=(flight, steps),
        in_specs=[
            pl.BlockSpec((1, nodes, double, wide), lambda e, s: (e, 0, 0, 0)),
            pl.BlockSpec((1, 1, rows, high), lambda e, s: (e, 0, 0, s)),
            pl.BlockSpec((1, 1, rows, hidden), lambda e, s: (e, 1, 0, 0)),
            pl.BlockSpec((1, nodes, double, low), lambda e, s: (e, 0, 0, s)),
        ],
        out_specs=(
            pl.BlockSpec((1, high, width), lambda e, s: (e, s, 0)),
            pl.BlockSpec((1, low, hidden), lambda e, s: (e, s, 0)),
        ),
        out_shape=(
            jax.ShapeDtypeStruct((flight, hidden, width), jnp.bfloat16),
            jax.ShapeDtypeStruct((flight, width, hidden), jnp.bfloat16),
        ),
        scratch_shapes=[pltpu.VMEM((rows, width), jnp.bfloat16)],
        compiler_params=pltpu.CompilerParams(vmem_limit_bytes=40 * 1024 * 1024),
        cost_estimate=pl.CostEstimate(
            flops=4 * flight * rows * width * hidden,
            bytes_accessed=4 * flight * width * hidden,
            transcendentals=0,
        ),
        name="weight_grads",
    )(rows_all, hidden_all, hidden_all, rows_all)


def local(tokens, upstream, router_probs, expert_ids, slot_index, w_in, w_out, router_weight):
    model_width = tokens.shape[1]
    flight, width = w_in.shape[:2]
    experts = router_probs.shape[1]
    nodes = lax.axis_size("node")
    locals_ = lax.axis_size("local")
    node = lax.axis_index("node")
    span = locals_ * CAP
    rows = nodes * span
    is_kept = slot_index >= 0
    target = jnp.where(is_kept, expert_ids * CAP + slot_index, -1)
    slot_iota = jnp.arange(flight * CAP, dtype=jnp.int32)
    slot_hits = slot_iota[:, None, None] == target[None, :, :]
    placing = jnp.any(slot_hits, axis=2).astype(jnp.bfloat16)
    high = router_probs.astype(jnp.bfloat16)
    low = (router_probs - high.astype(jnp.float32)).astype(jnp.bfloat16)
    room = jnp.zeros((high.shape[0], PAD // 2 - experts), jnp.bfloat16)
    probs = jnp.concatenate([high, room, low, room], axis=1)

    def place(array):
        return jnp.dot(placing, array, preferred_element_type=jnp.float32).astype(jnp.bfloat16)

    feats = jnp.stack(
        [place(tokens).reshape(flight, CAP, locals_, width),
         place(upstream).reshape(flight, CAP, locals_, width)], axis=1
    ).reshape(flight * 2 * CAP, locals_, width)
    tail = jnp.broadcast_to(
        place(probs).reshape(flight, 1, CAP, 1, PAD), (flight, 2, CAP, locals_, PAD)
    ).reshape(flight * 2 * CAP, locals_, PAD)
    send = jnp.swapaxes(jnp.concatenate([feats, tail], axis=2), 0, 1)

    rows_all, hidden_all, scores, home = run_exchange(send, w_in, w_out, nodes, locals_)
    w_out_grad, w_in_grad = weight_grads(rows_all, hidden_all, width)

    both = rows_all[:, :, 0:span, width:].reshape(flight, rows, 2, PAD // 2)[:, :, :, :experts]
    probs_rows = both[:, :, 0].astype(jnp.float32) + both[:, :, 1].astype(jnp.float32)
    own_prob = jnp.stack([probs_rows[e, :, e] for e in range(flight)])
    score = scores.reshape(flight, 8, rows)[:, 0, :, None]
    hot = (jnp.arange(experts)[None, :] == jnp.arange(flight)[:, None]).astype(jnp.float32)
    logit_rows = probs_rows * ((hot[:, None, :] - own_prob[:, :, None]) * score)
    logit_rows = logit_rows.astype(jnp.bfloat16)

    block = width // nodes
    picked = lax.dynamic_slice_in_dim(rows_all[:, :, 0:span], node * block, block, 3)
    part = contract(
        picked.reshape(flight * rows, block), logit_rows.reshape(flight * rows, experts), 0, 0
    )
    pairs = [
        (n * locals_ + l, nodes * l + n) for n in range(nodes) for l in range(locals_)
    ]
    router_grad = lax.ppermute(part, ("node", "local"), pairs)

    me = node * locals_ + lax.axis_index("local")
    home_logits = lax.dynamic_slice_in_dim(
        logit_rows.reshape(flight, nodes * locals_, CAP, experts), me, 1, 1
    )
    router_part = contract(home_logits.reshape(flight * CAP, experts), router_weight, 1, 1)
    home_rows = jnp.swapaxes(home, 0, 1).reshape(flight * CAP, model_width)
    total = (home_rows + router_part).astype(jnp.bfloat16)
    token_grads = contract(placing, total, 0, 0).astype(jnp.bfloat16)
    return (token_grads, w_in_grad, w_out_grad, router_grad)


def solution(mesh):
    in_specs = (
        P(("node", "local"), None),
        P(("node", "local"), None),
        P(("node", "local"), None),
        P(("node", "local"), None),
        P(("node", "local"), None),
        P(None, "local", "node"),
        P(None, "node", "local"),
        P(),
    )
    out_specs = (
        P(("node", "local"), None),
        P(None, "local", "node"),
        P(None, "node", "local"),
        P(("node", "local"), None),
    )
    return jax.shard_map(local, mesh=mesh, in_specs=in_specs, out_specs=out_specs, check_vma=False)
```

```python
import math

import jax
import jax.numpy as jnp
from jax import lax
from jax.experimental import pallas as pl
from jax.experimental.pallas import tpu as pltpu
from jax.sharding import PartitionSpec as P

CAP = 4
PAD = 128
MESH = pl.DeviceIdType.MESH
VMEM_BYTES = 60 * 1024 * 1024


root_two_pi = math.sqrt(2.0 / math.pi)
cubic_coef = 0.044715


def gelu_pair(pre):
    inner = root_two_pi * (pre + cubic_coef * pre * pre * pre)
    tangent = jnp.tanh(inner)
    value = 0.5 * pre * (1.0 + tangent)
    slope = 0.5 * (1.0 + tangent) + 0.5 * pre * (1.0 - tangent * tangent) * root_two_pi * (
        1.0 + 3.0 * cubic_coef * pre * pre
    )
    return (value, slope)


def contract(left, right, left_dim, right_dim):
    return lax.dot_general(
        left, right, (((left_dim,), (right_dim,)), ((), ())), preferred_element_type=jnp.float32
    )


def one_hot_rows(out_rows, in_rows, source):
    at = lax.broadcasted_iota(jnp.int32, (out_rows, in_rows), 0)
    column = lax.broadcasted_iota(jnp.int32, (out_rows, in_rows), 1)
    return (source(at) == column).astype(jnp.bfloat16)


def gate_column(blocks, expert):
    flat = blocks.reshape(-1, PAD).astype(jnp.float32)
    lane = lax.broadcasted_iota(jnp.int32, flat.shape, 1)
    return jnp.sum(jnp.where(lane == expert, flat, 0.0), axis=1, keepdims=True)


def exchange(dims, send, w_in, w_out, rows_out, hidden_out, part_out, logits_out, home_out,
             w_in_v, w_out_v, first, rows_v, part_s, part_r, own, hidden_v, terms, terms_r,
             core_sum, node_r, grads, home_s, home_r, score_1, score_2, score_3,
             w_sem, out_sem, a_s, a_r, z_s, z_r, c_s, c_r, p_s, p_r, g_s, g_r, t_s, t_r,
             n_s, n_r, h_s, h_r, s1_s, s1_r, s2_s, s2_r, s3_s, s3_r):
    nodes, locals_, flight, width, hidden = dims
    chips = nodes // 2
    span = locals_ * CAP
    rows = nodes * span
    piece = hidden // locals_
    node = lax.axis_index("node")
    loc = lax.axis_index("local")
    core = lax.rem(node, 2)
    chip = node // 2

    def local_peer(d):
        return (node, lax.rem(loc + d, locals_))

    def chip_peer(d):
        return (lax.rem(chip + d, chips) * 2 + core, loc)

    sibling = (chip * 2 + 1 - core, loc)
    peers = [local_peer(d) for d in range(1, locals_)]
    peers += [chip_peer(d) for d in range(1, chips)] + [sibling]

    def remote(src, dst, send_sem, recv_sem, peer):
        return pltpu.make_async_remote_copy(
            src_ref=src, dst_ref=dst, send_sem=send_sem, recv_sem=recv_sem,
            device_id=peer, device_id_type=MESH,
        )

    loads = []
    for e in range(flight):
        loads.append(pltpu.make_async_copy(w_in.at[e], w_in_v.at[e], w_sem.at[2 * e]))
        loads.append(pltpu.make_async_copy(w_out.at[e], w_out_v.at[e], w_sem.at[2 * e + 1]))
    for load in loads:
        load.start()

    barrier = pltpu.get_barrier_semaphore()
    for peer in peers:
        pl.semaphore_signal(barrier, inc=1, device_id=peer, device_id_type=MESH)
    pl.semaphore_wait(barrier, len(peers))

    sent = []

    def launch(copies):
        for copy in copies:
            copy.start()
        sent.extend(copies)
        return copies

    def arrive(copies):
        for copy in copies:
            copy.wait_recv()

    moved = launch([
        remote(send.at[lax.rem(loc + d, locals_)], first.at[loc], a_s.at[d], a_r.at[d], local_peer(d))
        for d in range(1, locals_)
    ])
    first[loc] = send[loc]
    arrive(moved)
    kinds = 2 * flight
    block = kinds * CAP

    def gather_source(i):
        k, rest = i // span, lax.rem(i, span)
        return (rest // CAP) * block + k * CAP + lax.rem(rest, CAP)

    order = one_hot_rows(kinds * span, locals_ * block, gather_source)
    ordered = contract(order, first[...].reshape(locals_ * block, width + PAD), 1, 0)
    ordered = ordered.astype(jnp.bfloat16)
    for e in range(flight):
        rows_v[e, node] = ordered[e * 2 * span:(e + 1) * 2 * span]

    def unit(u, at):
        return rows_v.at[u // 2, at, pl.ds((u % 2) * span, span)]

    def to_chips(u):
        copies = launch([
            remote(unit(u, node), unit(u, node), z_s.at[u, d], z_r.at[u, d], chip_peer(d))
            for d in range(1, chips)
        ])
        return copies, launch([
            remote(unit(u, node), unit(u, node), c_s.at[u, 0], c_r.at[u, 0], sibling)
        ])

    def finish_rows(u, moving):
        copies, over = moving
        for d in range(1, chips):
            copies[d - 1].wait_recv()
            at = lax.rem(chip + chips - d, chips) * 2 + core
            over = over + launch([
                remote(unit(u, at), unit(u, at), c_s.at[u, d], c_r.at[u, d], sibling)
            ])
        return over

    def project(u):
        e, kind = u // 2, u % 2
        loads[u].wait()
        left = rows_v[e, :, kind * span:(kind + 1) * span, 0:width].reshape(rows, width)
        copies = []
        tile = min(piece, 256)
        for d in list(range(1, locals_)) + [0]:
            base = lax.rem(loc + d, locals_) * piece

            def column(j, carry):
                at = pl.ds(pl.multiple_of(base + j * tile, tile), tile)
                to = pl.ds(pl.multiple_of(j * tile, tile), tile)
                if kind == 0:
                    made = contract(left, w_in_v[e, :, at], 1, 0)
                else:
                    made = contract(left, w_out_v[e, at, :], 1, 1)
                if d == 0:
                    own[e, kind, :, to] = made
                else:
                    part_s[e, d - 1, kind, :, to] = made.astype(jnp.bfloat16)
                return carry

            lax.fori_loop(0, piece // tile, column, 0)
            if d > 0:
                copies += launch([
                    remote(part_s.at[e, d - 1, kind], part_r.at[e, d - 1, kind], p_s.at[u, d],
                           p_r.at[u, d], local_peer(d))
                ])
        return copies

    here = pl.ds(pl.multiple_of(loc * piece, piece), piece)

    def spread_hidden(e, kind):
        mine = hidden_v.at[e, kind, :, here]
        return launch([
            remote(mine, mine, g_s.at[2 * e + kind, d], g_r.at[2 * e + kind, d], local_peer(d))
            for d in range(1, locals_)
        ])

    def hidden_step(e, copies):
        arrive(copies)
        gate = gate_column(rows_v[e, :, 0:span, width:width + PAD], e)
        pre, upw = own[e, 0], own[e, 1]
        for d in range(locals_ - 1):
            pre = pre + part_r[e, d, 0].astype(jnp.float32)
            upw = upw + part_r[e, d, 1].astype(jnp.float32)
        value, slope = gelu_pair(pre)
        act = value.astype(jnp.bfloat16)
        hidden_v[e, 0, :, here] = act
        hidden_v[e, 1, :, here] = (gate * upw * slope).astype(jnp.bfloat16)
        copies = spread_hidden(e, 1)
        score_1[loc, 8 * e:8 * e + 8] = lax.dot_general(
            jnp.ones((8, piece), jnp.float32), act.astype(jnp.float32) * upw,
            (((1,), (1,)), ((), ())), precision=lax.Precision.HIGHEST,
            preferred_element_type=jnp.float32,
        )
        return copies

    def row_terms(e, copies):
        arrive(copies)
        tile = min(width, 512)

        def column(j, carry):
            at = pl.ds(pl.multiple_of(j * tile, tile), tile)
            made = contract(hidden_v[e, 1], w_in_v[e, at, :], 1, 1).astype(jnp.bfloat16)
            terms[e, :, :, :, at] = made.reshape(chips, 2, span, tile)
            return carry

        lax.fori_loop(0, width // tile, column, 0)
        return launch([
            remote(terms.at[e, :, 1 - core], terms_r.at[e], t_s.at[e], t_r.at[e], sibling)
        ])

    def reduce_nodes(e, copies):
        arrive(copies)
        core_sum[e] = (
            terms[e, :, core].astype(jnp.float32) + terms_r[e].astype(jnp.float32)
        ).astype(jnp.bfloat16)
        return launch([
            remote(core_sum.at[e, lax.rem(chip + d, chips)], node_r.at[e, d - 1], n_s.at[e, d],
                   n_r.at[e, d], chip_peer(d))
            for d in range(1, chips)
        ])

    def finish_grads(e, copies):
        arrive(copies)
        total = core_sum[e, chip].astype(jnp.float32)
        for d in range(chips - 1):
            total = total + node_r[e, d].astype(jnp.float32)
        grads[e] = total.astype(jnp.bfloat16)

    def logits(total):
        made = jnp.zeros(part_out.shape, jnp.float32)
        me = node * locals_ + loc
        mine = one_hot_rows(8, rows, lambda i: me * CAP + i)
        fold = one_hot_rows(PAD, PAD, lambda i: lax.rem(i, PAD // 2))
        span_out = part_out.shape[0]
        for e in range(flight):
            flat = rows_v[e, :, 0:span, width:width + PAD].reshape(rows, PAD)
            probs = contract(flat, fold, 1, 0)
            lane = lax.broadcasted_iota(jnp.int32, (rows, PAD), 1)
            own_prob = jnp.sum(jnp.where(lane == e, probs, 0.0), axis=1, keepdims=True)
            line = lax.broadcasted_iota(jnp.int32, (8 * flight, PAD), 0)
            score = lax.dot_general(
                total, (line == 8 * e).astype(jnp.float32), (((0,), (0,)), ((), ())),
                precision=lax.Precision.HIGHEST, preferred_element_type=jnp.float32,
            )
            hot = (lane == e).astype(jnp.float32)
            logit = (probs * ((hot - own_prob) * score)).astype(jnp.bfloat16)
            logits_out[8 * e:8 * e + 8] = contract(mine, logit, 1, 0)
            if span_out % 128 == 0:
                at = pl.ds(pl.multiple_of(node * span_out, span_out), span_out)
                picked = rows_v[e, :, 0:span, at].reshape(rows, span_out)
            else:
                left = rows_v[e, :, 0:span, 0:width].reshape(rows, width)
                line = lax.broadcasted_iota(jnp.int32, (width, span_out), 0)
                lane = lax.broadcasted_iota(jnp.int32, (width, span_out), 1)
                chosen = (line == lane + node * span_out).astype(jnp.bfloat16)
                picked = contract(left, chosen, 1, 0).astype(jnp.bfloat16)
            made = made + contract(picked, logit, 0, 0)
        part_out[...] = made

    over = finish_rows(0, to_chips(0))
    moving = to_chips(1)
    arrive(over)
    parts_0 = project(0)
    over = finish_rows(1, moving)
    moving = to_chips(2)
    arrive(over)
    parts_0 += project(1)
    over = finish_rows(2, moving)
    moving = to_chips(3)
    arrive(over)
    parts_1 = project(2)
    hidden_0 = hidden_step(0, parts_0)
    over = finish_rows(3, moving)
    arrive(over)
    rows_copy = pltpu.make_async_copy(rows_v, rows_out, out_sem.at[0])
    rows_copy.start()
    parts_1 += project(3)
    terms_0 = row_terms(0, hidden_0)
    hidden_1 = hidden_step(1, parts_1)

    near = launch([
        remote(score_1.at[loc], score_1.at[loc], s1_s.at[d], s1_r.at[d], local_peer(d))
        for d in range(1, locals_)
    ])
    nodes_0 = reduce_nodes(0, terms_0)
    arrive(near)
    score_2[chip] = jnp.sum(score_1[...], axis=0)
    along = launch([
        remote(score_2.at[chip], score_2.at[chip], s2_s.at[d], s2_r.at[d], chip_peer(d))
        for d in range(1, chips)
    ])
    arrive(hidden_1)
    acts = spread_hidden(0, 0) + spread_hidden(1, 0)
    terms_1 = row_terms(1, [])
    grad_copy = pltpu.make_async_copy(hidden_v.at[:, 1], hidden_out.at[1], out_sem.at[1])
    grad_copy.start()
    arrive(along)
    score_3[core] = jnp.sum(score_2[...], axis=0)
    across = launch([
        remote(score_3.at[core], score_3.at[core], s3_s.at[0], s3_r.at[0], sibling)
    ])
    nodes_1 = reduce_nodes(1, terms_1)
    finish_grads(0, nodes_0)
    arrive(across)
    logits(score_3[0] + score_3[1])
    finish_grads(1, nodes_1)

    def home_source(i):
        at, rest = i // (flight * CAP), lax.rem(i, flight * CAP)
        return (rest // CAP) * span + at * CAP + lax.rem(rest, CAP)

    pick = one_hot_rows(locals_ * flight * CAP, flight * span, home_source)
    picked = contract(pick, grads[...].reshape(flight * span, width), 1, 0)
    home_s[...] = picked.reshape(locals_, flight * CAP, width)
    home = launch([
        remote(home_s.at[lax.rem(loc + d, locals_)], home_r.at[loc], h_s.at[d], h_r.at[d],
               local_peer(d))
        for d in range(1, locals_)
    ])
    home_r[loc] = home_s[loc]
    arrive(acts)
    act_copy = pltpu.make_async_copy(hidden_v.at[:, 0], hidden_out.at[0], out_sem.at[2])
    act_copy.start()
    arrive(home)
    home_out[...] = home_r[...]
    for copy in sent:
        copy.wait_send()
    rows_copy.wait()
    grad_copy.wait()
    act_copy.wait()


def run_exchange(send, w_in, w_out, nodes, locals_):
    flight, width, hidden = w_in.shape
    chips = nodes // 2
    span = locals_ * CAP
    rows = nodes * span
    piece = hidden // locals_
    wide = width + PAD
    block = send.shape[1]
    half, full = jnp.bfloat16, jnp.float32
    dma = pltpu.SemaphoreType.DMA
    vmem = pl.BlockSpec(memory_space=pltpu.VMEM)
    hbm = pl.BlockSpec(memory_space=pl.ANY)

    def kernel(*refs):
        exchange((nodes, locals_, flight, width, hidden), *refs)

    return pl.pallas_call(
        kernel,
        out_shape=(
            jax.ShapeDtypeStruct((flight, nodes, 2 * span, wide), half),
            jax.ShapeDtypeStruct((2, flight, rows, hidden), half),
            jax.ShapeDtypeStruct((width // nodes, PAD), full),
            jax.ShapeDtypeStruct((flight * 8, PAD), full),
            jax.ShapeDtypeStruct((locals_, flight * CAP, width), full),
        ),
        in_specs=[vmem, hbm, hbm],
        out_specs=(hbm, hbm, vmem, vmem, vmem),
        scratch_shapes=[
            pltpu.VMEM((flight, width, hidden), half),
            pltpu.VMEM((flight, hidden, width), half),
            pltpu.VMEM((locals_, block, wide), half),
            pltpu.VMEM((flight, nodes, 2 * span, wide), half),
            pltpu.VMEM((flight, locals_ - 1, 2, rows, piece), half),
            pltpu.VMEM((flight, locals_ - 1, 2, rows, piece), half),
            pltpu.VMEM((flight, 2, rows, piece), full),
            pltpu.VMEM((flight, 2, rows, hidden), half),
            pltpu.VMEM((flight, chips, 2, span, width), half),
            pltpu.VMEM((flight, chips, span, width), half),
            pltpu.VMEM((flight, chips, span, width), half),
            pltpu.VMEM((flight, chips - 1, span, width), half),
            pltpu.VMEM((flight, span, width), half),
            pltpu.VMEM((locals_, flight * CAP, width), full),
            pltpu.VMEM((locals_, flight * CAP, width), full),
            pltpu.VMEM((locals_, flight * 8, rows), full),
            pltpu.VMEM((chips, flight * 8, rows), full),
            pltpu.VMEM((2, flight * 8, rows), full),
            dma((2 * flight,)), dma((3,)),
            dma((locals_,)), dma((locals_,)),
            dma((2 * flight, chips)), dma((2 * flight, chips)),
            dma((2 * flight, chips)), dma((2 * flight, chips)),
            dma((2 * flight, locals_)), dma((2 * flight, locals_)),
            dma((2 * flight, locals_)), dma((2 * flight, locals_)),
            dma((flight,)), dma((flight,)),
            dma((flight, chips)), dma((flight, chips)),
            dma((locals_,)), dma((locals_,)),
            dma((locals_,)), dma((locals_,)),
            dma((chips,)), dma((chips,)),
            dma((1,)), dma((1,)),
        ],
        compiler_params=pltpu.CompilerParams(
            collective_id=0, has_side_effects=True, vmem_limit_bytes=VMEM_BYTES
        ),
        cost_estimate=pl.CostEstimate(
            flops=6 * flight * rows * width * hidden,
            bytes_accessed=4 * flight * width * hidden,
            transcendentals=flight * rows * piece,
        ),
        name="exchange",
    )(send, w_in, w_out)


def weight_grads(rows_all, hidden_all, width):
    flight, nodes, double, wide = rows_all.shape
    span = double // 2
    rows, hidden = hidden_all.shape[2:]
    steps = 4
    high, low = hidden // steps, width // steps

    def kernel(rows_ref, act_ref, grad_ref, left_ref, out_ref, in_ref, out_grad):
        e, step = pl.program_id(0), pl.program_id(1)

        @pl.when(step == 0)
        def _():
            gate = gate_column(rows_ref[0, :, 0:span, width:wide], e)
            up = rows_ref[0, :, span:double, 0:width].reshape(rows, width)
            out_grad[...] = (gate * up.astype(jnp.float32)).astype(jnp.bfloat16)

        out_ref[0] = contract(act_ref[0, 0], out_grad[...], 0, 0).astype(jnp.bfloat16)
        left = left_ref[0, :, 0:span].reshape(rows, low)
        in_ref[0] = contract(left, grad_ref[0, 0], 0, 0).astype(jnp.bfloat16)

    return pl.pallas_call(
        kernel,
        grid=(flight, steps),
        in_specs=[
            pl.BlockSpec((1, nodes, double, wide), lambda e, s: (e, 0, 0, 0)),
            pl.BlockSpec((1, 1, rows, high), lambda e, s: (0, e, 0, s)),
            pl.BlockSpec((1, 1, rows, hidden), lambda e, s: (1, e, 0, 0)),
            pl.BlockSpec((1, nodes, double, low), lambda e, s: (e, 0, 0, s)),
        ],
        out_specs=(
            pl.BlockSpec((1, high, width), lambda e, s: (e, s, 0)),
            pl.BlockSpec((1, low, hidden), lambda e, s: (e, s, 0)),
        ),
        out_shape=(
            jax.ShapeDtypeStruct((flight, hidden, width), jnp.bfloat16),
            jax.ShapeDtypeStruct((flight, width, hidden), jnp.bfloat16),
        ),
        scratch_shapes=[pltpu.VMEM((rows, width), jnp.bfloat16)],
        compiler_params=pltpu.CompilerParams(vmem_limit_bytes=40 * 1024 * 1024),
        cost_estimate=pl.CostEstimate(
            flops=4 * flight * rows * width * hidden,
            bytes_accessed=4 * flight * width * hidden,
            transcendentals=0,
        ),
        name="weight_grads",
    )(rows_all, hidden_all, hidden_all, rows_all)


def local(tokens, upstream, router_probs, expert_ids, slot_index, w_in, w_out, router_weight):
    model_width = tokens.shape[1]
    flight, width = w_in.shape[:2]
    experts = router_probs.shape[1]
    nodes = lax.axis_size("node")
    locals_ = lax.axis_size("local")
    is_kept = slot_index >= 0
    target = jnp.where(is_kept, expert_ids * CAP + slot_index, -1)
    slot_iota = jnp.arange(flight * CAP, dtype=jnp.int32)
    slot_hits = slot_iota[:, None, None] == target[None, :, :]
    placing = jnp.any(slot_hits, axis=2).astype(jnp.bfloat16)
    high = router_probs.astype(jnp.bfloat16)
    low = (router_probs - high.astype(jnp.float32)).astype(jnp.bfloat16)
    room = jnp.zeros((high.shape[0], PAD // 2 - experts), jnp.bfloat16)
    probs = jnp.concatenate([high, room, low, room], axis=1)

    def place(array):
        return jnp.dot(placing, array, preferred_element_type=jnp.float32).astype(jnp.bfloat16)

    feats = jnp.stack(
        [place(tokens).reshape(flight, CAP, locals_, width),
         place(upstream).reshape(flight, CAP, locals_, width)], axis=1
    ).reshape(flight * 2 * CAP, locals_, width)
    tail = jnp.broadcast_to(
        place(probs).reshape(flight, 1, CAP, 1, PAD), (flight, 2, CAP, locals_, PAD)
    ).reshape(flight * 2 * CAP, locals_, PAD)
    send = jnp.swapaxes(jnp.concatenate([feats, tail], axis=2), 0, 1)

    rows_all, hidden_all, part, logits, home = run_exchange(send, w_in, w_out, nodes, locals_)

    pairs = [
        (n * locals_ + l, nodes * l + n) for n in range(nodes) for l in range(locals_)
    ]
    router_grad = lax.ppermute(part[:, :experts], ("node", "local"), pairs)
    w_out_grad, w_in_grad = weight_grads(rows_all, hidden_all, width)
    home_logits = logits.reshape(flight, 8, PAD)[:, :CAP, :experts].astype(jnp.bfloat16)
    router_part = contract(home_logits.reshape(flight * CAP, experts), router_weight, 1, 1)
    home_rows = jnp.swapaxes(home, 0, 1).reshape(flight * CAP, model_width)
    total = (home_rows + router_part).astype(jnp.bfloat16)
    token_grads = contract(placing, total, 0, 0).astype(jnp.bfloat16)
    return (token_grads, w_in_grad, w_out_grad, router_grad)


def solution(mesh):
    in_specs = (
        P(("node", "local"), None),
        P(("node", "local"), None),
        P(("node", "local"), None),
        P(("node", "local"), None),
        P(("node", "local"), None),
        P(None, "local", "node"),
        P(None, "node", "local"),
        P(),
    )
    out_specs = (
        P(("node", "local"), None),
        P(None, "local", "node"),
        P(None, "node", "local"),
        P(("node", "local"), None),
    )
    return jax.shard_map(local, mesh=mesh, in_specs=in_specs, out_specs=out_specs, check_vma=False)
```

```python
import math

import jax
import jax.numpy as jnp
from jax import lax
from jax.experimental import pallas as pl
from jax.experimental.pallas import tpu as pltpu
from jax.sharding import PartitionSpec as P

CAP = 4
PAD = 128
MESH = pl.DeviceIdType.MESH
VMEM_BYTES = 60 * 1024 * 1024


root_two_pi = math.sqrt(2.0 / math.pi)
cubic_coef = 0.044715


def gelu_pair(pre):
    inner = root_two_pi * (pre + cubic_coef * pre * pre * pre)
    tangent = jnp.tanh(inner)
    value = 0.5 * pre * (1.0 + tangent)
    slope = 0.5 * (1.0 + tangent) + 0.5 * pre * (1.0 - tangent * tangent) * root_two_pi * (
        1.0 + 3.0 * cubic_coef * pre * pre
    )
    return (value, slope)


def contract(left, right, left_dim, right_dim):
    return lax.dot_general(
        left, right, (((left_dim,), (right_dim,)), ((), ())), preferred_element_type=jnp.float32
    )


def one_hot_rows(out_rows, in_rows, source):
    at = lax.broadcasted_iota(jnp.int32, (out_rows, in_rows), 0)
    column = lax.broadcasted_iota(jnp.int32, (out_rows, in_rows), 1)
    return (source(at) == column).astype(jnp.bfloat16)


def gate_column(blocks, expert):
    flat = blocks.reshape(-1, PAD).astype(jnp.float32)
    lane = lax.broadcasted_iota(jnp.int32, flat.shape, 1)
    return jnp.sum(jnp.where(lane == expert, flat, 0.0), axis=1, keepdims=True)


def exchange(dims, send, w_in, w_out, rows_out, hidden_out, part_out, logits_out, home_out,
             w_in_v, w_out_v, first, rows_v, part_s, part_r, own, hidden_v, terms, terms_r,
             core_sum, node_r, grads, home_s, home_r, score_1, score_2, score_3,
             w_sem, out_sem, a_s, a_r, z_s, z_r, c_s, c_r, p_s, p_r, g_s, g_r, t_s, t_r,
             n_s, n_r, h_s, h_r, s1_s, s1_r, s2_s, s2_r, s3_s, s3_r):
    nodes, locals_, flight, width, hidden = dims
    chips = nodes // 2
    span = locals_ * CAP
    rows = nodes * span
    piece = hidden // locals_
    node = lax.axis_index("node")
    loc = lax.axis_index("local")
    core = lax.rem(node, 2)
    chip = node // 2

    def local_peer(d):
        return (node, lax.rem(loc + d, locals_))

    def chip_peer(d):
        return (lax.rem(chip + d, chips) * 2 + core, loc)

    sibling = (chip * 2 + 1 - core, loc)
    peers = [local_peer(d) for d in range(1, locals_)]
    peers += [chip_peer(d) for d in range(1, chips)] + [sibling]

    def remote(src, dst, send_sem, recv_sem, peer):
        return pltpu.make_async_remote_copy(
            src_ref=src, dst_ref=dst, send_sem=send_sem, recv_sem=recv_sem,
            device_id=peer, device_id_type=MESH,
        )

    loads = []
    for e in range(flight):
        loads.append(pltpu.make_async_copy(w_in.at[e], w_in_v.at[e], w_sem.at[2 * e]))
        loads.append(pltpu.make_async_copy(w_out.at[e], w_out_v.at[e], w_sem.at[2 * e + 1]))
    for load in loads:
        load.start()

    barrier = pltpu.get_barrier_semaphore()
    for peer in peers:
        pl.semaphore_signal(barrier, inc=1, device_id=peer, device_id_type=MESH)
    pl.semaphore_wait(barrier, len(peers))

    sent = []

    def launch(copies):
        for copy in copies:
            copy.start()
        sent.extend(copies)
        return copies

    def arrive(copies):
        for copy in copies:
            copy.wait_recv()

    moved = launch([
        remote(send.at[lax.rem(loc + d, locals_)], first.at[loc], a_s.at[d], a_r.at[d], local_peer(d))
        for d in range(1, locals_)
    ])
    first[loc] = send[loc]
    arrive(moved)
    kinds = 2 * flight
    block = kinds * CAP

    def gather_source(i):
        k, rest = i // span, lax.rem(i, span)
        return (rest // CAP) * block + k * CAP + lax.rem(rest, CAP)

    order = one_hot_rows(kinds * span, locals_ * block, gather_source)
    ordered = contract(order, first[...].reshape(locals_ * block, width + PAD), 1, 0)
    ordered = ordered.astype(jnp.bfloat16)
    for e in range(flight):
        rows_v[e, node] = ordered[e * 2 * span:(e + 1) * 2 * span]

    def unit(u, at):
        return rows_v.at[u // 2, at, pl.ds((u % 2) * span, span)]

    def to_chips(u):
        copies = launch([
            remote(unit(u, node), unit(u, node), z_s.at[u, d], z_r.at[u, d], chip_peer(d))
            for d in range(1, chips)
        ])
        return copies, launch([
            remote(unit(u, node), unit(u, node), c_s.at[u, 0], c_r.at[u, 0], sibling)
        ])

    def finish_rows(u, moving):
        copies, over = moving
        for d in range(1, chips):
            copies[d - 1].wait_recv()
            at = lax.rem(chip + chips - d, chips) * 2 + core
            over = over + launch([
                remote(unit(u, at), unit(u, at), c_s.at[u, d], c_r.at[u, d], sibling)
            ])
        return over

    def project(u):
        e, kind = u // 2, u % 2
        loads[u].wait()
        left = rows_v[e, :, kind * span:(kind + 1) * span, 0:width].reshape(rows, width)
        copies = []
        tile = min(piece, 256)
        for d in list(range(1, locals_)) + [0]:
            base = lax.rem(loc + d, locals_) * piece

            def column(j, carry):
                at = pl.ds(pl.multiple_of(base + j * tile, tile), tile)
                to = pl.ds(pl.multiple_of(j * tile, tile), tile)
                if kind == 0:
                    made = contract(left, w_in_v[e, :, at], 1, 0)
                else:
                    made = contract(left, w_out_v[e, at, :], 1, 1)
                if d == 0:
                    own[e, kind, :, to] = made
                else:
                    part_s[e, d - 1, kind, :, to] = made.astype(jnp.bfloat16)
                return carry

            lax.fori_loop(0, piece // tile, column, 0)
            if d > 0:
                copies += launch([
                    remote(part_s.at[e, d - 1, kind], part_r.at[e, d - 1, kind], p_s.at[u, d],
                           p_r.at[u, d], local_peer(d))
                ])
        return copies

    here = pl.ds(pl.multiple_of(loc * piece, piece), piece)

    def spread_hidden(e, kind):
        mine = hidden_v.at[e, kind, :, here]
        return launch([
            remote(mine, mine, g_s.at[2 * e + kind, d], g_r.at[2 * e + kind, d], local_peer(d))
            for d in range(1, locals_)
        ])

    def hidden_step(e, copies):
        arrive(copies)
        gate = gate_column(rows_v[e, :, 0:span, width:width + PAD], e)
        pre, upw = own[e, 0], own[e, 1]
        for d in range(locals_ - 1):
            pre = pre + part_r[e, d, 0].astype(jnp.float32)
            upw = upw + part_r[e, d, 1].astype(jnp.float32)
        value, slope = gelu_pair(pre)
        act = value.astype(jnp.bfloat16)
        hidden_v[e, 0, :, here] = act
        hidden_v[e, 1, :, here] = (gate * upw * slope).astype(jnp.bfloat16)
        copies = spread_hidden(e, 1)
        score_1[loc, 8 * e:8 * e + 8] = lax.dot_general(
            jnp.ones((8, piece), jnp.float32), act.astype(jnp.float32) * upw,
            (((1,), (1,)), ((), ())), precision=lax.Precision.HIGHEST,
            preferred_element_type=jnp.float32,
        )
        return copies

    half_width = width // 2

    def row_terms(e, h):
        tile = min(half_width, 512)

        def column(j, carry):
            at = pl.ds(pl.multiple_of(h * half_width + j * tile, tile), tile)
            made = contract(hidden_v[e, 1], w_in_v[e, at, :], 1, 1).astype(jnp.bfloat16)
            terms[e, :, :, :, at] = made.reshape(chips, 2, span, tile)
            return carry

        lax.fori_loop(0, half_width // tile, column, 0)
        cut = pl.ds(h * half_width, half_width)
        return launch([
            remote(terms.at[e, :, 1 - core, :, cut], terms_r.at[e, :, :, cut], t_s.at[2 * e + h],
                   t_r.at[2 * e + h], sibling)
        ])

    def reduce_nodes(e, h, copies):
        arrive(copies)
        cut = pl.ds(h * half_width, half_width)
        core_sum[e, :, :, cut] = (
            terms[e, :, core, :, cut].astype(jnp.float32)
            + terms_r[e, :, :, cut].astype(jnp.float32)
        ).astype(jnp.bfloat16)
        return launch([
            remote(core_sum.at[e, lax.rem(chip + d, chips), :, cut], node_r.at[e, d - 1, :, cut],
                   n_s.at[2 * e + h, d], n_r.at[2 * e + h, d], chip_peer(d))
            for d in range(1, chips)
        ])

    def finish_grads(e, h, copies):
        arrive(copies)
        cut = pl.ds(h * half_width, half_width)
        total = core_sum[e, chip, :, cut].astype(jnp.float32)
        for d in range(chips - 1):
            total = total + node_r[e, d, :, cut].astype(jnp.float32)
        grads[e, :, cut] = total.astype(jnp.bfloat16)

    def home_source(i):
        at, rest = i // (flight * CAP), lax.rem(i, flight * CAP)
        return (rest // CAP) * span + at * CAP + lax.rem(rest, CAP)

    def send_home(h):
        cut = pl.ds(h * half_width, half_width)
        pick = one_hot_rows(locals_ * flight * CAP, flight * span, home_source)
        picked = contract(pick, grads[:, :, cut].reshape(flight * span, half_width), 1, 0)
        home_s[:, :, cut] = picked.reshape(locals_, flight * CAP, half_width)
        copies = launch([
            remote(home_s.at[lax.rem(loc + d, locals_), :, cut], home_r.at[loc, :, cut],
                   h_s.at[h, d], h_r.at[h, d], local_peer(d))
            for d in range(1, locals_)
        ])
        home_r[loc, :, cut] = home_s[loc, :, cut]
        return copies

    def logits(total):
        made = jnp.zeros(part_out.shape, jnp.float32)
        me = node * locals_ + loc
        mine = one_hot_rows(8, rows, lambda i: me * CAP + i)
        fold = one_hot_rows(PAD, PAD, lambda i: lax.rem(i, PAD // 2))
        span_out = part_out.shape[0]
        for e in range(flight):
            flat = rows_v[e, :, 0:span, width:width + PAD].reshape(rows, PAD)
            probs = contract(flat, fold, 1, 0)
            lane = lax.broadcasted_iota(jnp.int32, (rows, PAD), 1)
            own_prob = jnp.sum(jnp.where(lane == e, probs, 0.0), axis=1, keepdims=True)
            line = lax.broadcasted_iota(jnp.int32, (8 * flight, PAD), 0)
            score = lax.dot_general(
                total, (line == 8 * e).astype(jnp.float32), (((0,), (0,)), ((), ())),
                precision=lax.Precision.HIGHEST, preferred_element_type=jnp.float32,
            )
            hot = (lane == e).astype(jnp.float32)
            logit = (probs * ((hot - own_prob) * score)).astype(jnp.bfloat16)
            logits_out[8 * e:8 * e + 8] = contract(mine, logit, 1, 0)
            if span_out % 128 == 0:
                at = pl.ds(pl.multiple_of(node * span_out, span_out), span_out)
                picked = rows_v[e, :, 0:span, at].reshape(rows, span_out)
            else:
                left = rows_v[e, :, 0:span, 0:width].reshape(rows, width)
                line = lax.broadcasted_iota(jnp.int32, (width, span_out), 0)
                lane = lax.broadcasted_iota(jnp.int32, (width, span_out), 1)
                chosen = (line == lane + node * span_out).astype(jnp.bfloat16)
                picked = contract(left, chosen, 1, 0).astype(jnp.bfloat16)
            made = made + contract(picked, logit, 0, 0)
        part_out[...] = made

    over = finish_rows(0, to_chips(0))
    moving = to_chips(1)
    arrive(over)
    parts_0 = project(0)
    over = finish_rows(1, moving)
    moving = to_chips(2)
    arrive(over)
    parts_0 += project(1)
    over = finish_rows(2, moving)
    moving = to_chips(3)
    arrive(over)
    parts_1 = project(2)
    hidden_0 = hidden_step(0, parts_0)
    over = finish_rows(3, moving)
    arrive(over)
    rows_copy = pltpu.make_async_copy(rows_v, rows_out, out_sem.at[0])
    rows_copy.start()
    parts_1 += project(3)
    arrive(hidden_0)
    terms_0 = [row_terms(0, h) for h in range(2)]
    hidden_1 = hidden_step(1, parts_1)

    near = launch([
        remote(score_1.at[loc], score_1.at[loc], s1_s.at[d], s1_r.at[d], local_peer(d))
        for d in range(1, locals_)
    ])
    nodes_0 = [reduce_nodes(0, h, terms_0[h]) for h in range(2)]
    arrive(near)
    score_2[chip] = jnp.sum(score_1[...], axis=0)
    along = launch([
        remote(score_2.at[chip], score_2.at[chip], s2_s.at[d], s2_r.at[d], chip_peer(d))
        for d in range(1, chips)
    ])
    arrive(hidden_1)
    acts = spread_hidden(0, 0) + spread_hidden(1, 0)
    terms_1 = [row_terms(1, h) for h in range(2)]
    nodes_1 = [reduce_nodes(1, 0, terms_1[0])]
    grad_copy = pltpu.make_async_copy(hidden_v.at[:, 1], hidden_out.at[1], out_sem.at[1])
    grad_copy.start()
    arrive(along)
    score_3[core] = jnp.sum(score_2[...], axis=0)
    across = launch([
        remote(score_3.at[core], score_3.at[core], s3_s.at[0], s3_r.at[0], sibling)
    ])
    nodes_1 += [reduce_nodes(1, 1, terms_1[1])]
    for h in range(2):
        finish_grads(0, h, nodes_0[h])
    arrive(across)
    logits(score_3[0] + score_3[1])
    home = []
    for h in range(2):
        finish_grads(1, h, nodes_1[h])
        home += send_home(h)
    arrive(acts)
    act_copy = pltpu.make_async_copy(hidden_v.at[:, 0], hidden_out.at[0], out_sem.at[2])
    act_copy.start()
    arrive(home)
    home_out[...] = home_r[...]
    for copy in sent:
        copy.wait_send()
    rows_copy.wait()
    grad_copy.wait()
    act_copy.wait()


def run_exchange(send, w_in, w_out, nodes, locals_):
    flight, width, hidden = w_in.shape
    chips = nodes // 2
    span = locals_ * CAP
    rows = nodes * span
    piece = hidden // locals_
    wide = width + PAD
    block = send.shape[1]
    half, full = jnp.bfloat16, jnp.float32
    dma = pltpu.SemaphoreType.DMA
    vmem = pl.BlockSpec(memory_space=pltpu.VMEM)
    hbm = pl.BlockSpec(memory_space=pl.ANY)

    def kernel(*refs):
        exchange((nodes, locals_, flight, width, hidden), *refs)

    return pl.pallas_call(
        kernel,
        out_shape=(
            jax.ShapeDtypeStruct((flight, nodes, 2 * span, wide), half),
            jax.ShapeDtypeStruct((2, flight, rows, hidden), half),
            jax.ShapeDtypeStruct((width // nodes, PAD), full),
            jax.ShapeDtypeStruct((flight * 8, PAD), full),
            jax.ShapeDtypeStruct((locals_, flight * CAP, width), full),
        ),
        in_specs=[vmem, hbm, hbm],
        out_specs=(hbm, hbm, vmem, vmem, vmem),
        scratch_shapes=[
            pltpu.VMEM((flight, width, hidden), half),
            pltpu.VMEM((flight, hidden, width), half),
            pltpu.VMEM((locals_, block, wide), half),
            pltpu.VMEM((flight, nodes, 2 * span, wide), half),
            pltpu.VMEM((flight, locals_ - 1, 2, rows, piece), half),
            pltpu.VMEM((flight, locals_ - 1, 2, rows, piece), half),
            pltpu.VMEM((flight, 2, rows, piece), full),
            pltpu.VMEM((flight, 2, rows, hidden), half),
            pltpu.VMEM((flight, chips, 2, span, width), half),
            pltpu.VMEM((flight, chips, span, width), half),
            pltpu.VMEM((flight, chips, span, width), half),
            pltpu.VMEM((flight, chips - 1, span, width), half),
            pltpu.VMEM((flight, span, width), half),
            pltpu.VMEM((locals_, flight * CAP, width), full),
            pltpu.VMEM((locals_, flight * CAP, width), full),
            pltpu.VMEM((locals_, flight * 8, rows), full),
            pltpu.VMEM((chips, flight * 8, rows), full),
            pltpu.VMEM((2, flight * 8, rows), full),
            dma((2 * flight,)), dma((3,)),
            dma((locals_,)), dma((locals_,)),
            dma((2 * flight, chips)), dma((2 * flight, chips)),
            dma((2 * flight, chips)), dma((2 * flight, chips)),
            dma((2 * flight, locals_)), dma((2 * flight, locals_)),
            dma((2 * flight, locals_)), dma((2 * flight, locals_)),
            dma((2 * flight,)), dma((2 * flight,)),
            dma((2 * flight, chips)), dma((2 * flight, chips)),
            dma((2, locals_)), dma((2, locals_)),
            dma((locals_,)), dma((locals_,)),
            dma((chips,)), dma((chips,)),
            dma((1,)), dma((1,)),
        ],
        compiler_params=pltpu.CompilerParams(
            collective_id=0, has_side_effects=True, vmem_limit_bytes=VMEM_BYTES
        ),
        cost_estimate=pl.CostEstimate(
            flops=6 * flight * rows * width * hidden,
            bytes_accessed=4 * flight * width * hidden,
            transcendentals=flight * rows * piece,
        ),
        name="exchange",
    )(send, w_in, w_out)


def weight_grads(rows_all, hidden_all, width):
    flight, nodes, double, wide = rows_all.shape
    span = double // 2
    rows, hidden = hidden_all.shape[2:]
    steps = 4
    high, low = hidden // steps, width // steps

    def kernel(rows_ref, act_ref, grad_ref, left_ref, out_ref, in_ref, out_grad):
        e, step = pl.program_id(0), pl.program_id(1)

        @pl.when(step == 0)
        def _():
            gate = gate_column(rows_ref[0, :, 0:span, width:wide], e)
            up = rows_ref[0, :, span:double, 0:width].reshape(rows, width)
            out_grad[...] = (gate * up.astype(jnp.float32)).astype(jnp.bfloat16)

        out_ref[0] = contract(act_ref[0, 0], out_grad[...], 0, 0).astype(jnp.bfloat16)
        left = left_ref[0, :, 0:span].reshape(rows, low)
        in_ref[0] = contract(left, grad_ref[0, 0], 0, 0).astype(jnp.bfloat16)

    return pl.pallas_call(
        kernel,
        grid=(flight, steps),
        in_specs=[
            pl.BlockSpec((1, nodes, double, wide), lambda e, s: (e, 0, 0, 0)),
            pl.BlockSpec((1, 1, rows, high), lambda e, s: (0, e, 0, s)),
            pl.BlockSpec((1, 1, rows, hidden), lambda e, s: (1, e, 0, 0)),
            pl.BlockSpec((1, nodes, double, low), lambda e, s: (e, 0, 0, s)),
        ],
        out_specs=(
            pl.BlockSpec((1, high, width), lambda e, s: (e, s, 0)),
            pl.BlockSpec((1, low, hidden), lambda e, s: (e, s, 0)),
        ),
        out_shape=(
            jax.ShapeDtypeStruct((flight, hidden, width), jnp.bfloat16),
            jax.ShapeDtypeStruct((flight, width, hidden), jnp.bfloat16),
        ),
        scratch_shapes=[pltpu.VMEM((rows, width), jnp.bfloat16)],
        compiler_params=pltpu.CompilerParams(vmem_limit_bytes=VMEM_BYTES),
        cost_estimate=pl.CostEstimate(
            flops=4 * flight * rows * width * hidden,
            bytes_accessed=4 * flight * width * hidden,
            transcendentals=0,
        ),
        name="weight_grads",
    )(rows_all, hidden_all, hidden_all, rows_all)


def local(tokens, upstream, router_probs, expert_ids, slot_index, w_in, w_out, router_weight):
    model_width = tokens.shape[1]
    flight, width = w_in.shape[:2]
    experts = router_probs.shape[1]
    nodes = lax.axis_size("node")
    locals_ = lax.axis_size("local")
    is_kept = slot_index >= 0
    target = jnp.where(is_kept, expert_ids * CAP + slot_index, -1)
    slot_iota = jnp.arange(flight * CAP, dtype=jnp.int32)
    slot_hits = slot_iota[:, None, None] == target[None, :, :]
    placing = jnp.any(slot_hits, axis=2).astype(jnp.bfloat16)
    high = router_probs.astype(jnp.bfloat16)
    low = (router_probs - high.astype(jnp.float32)).astype(jnp.bfloat16)
    room = jnp.zeros((high.shape[0], PAD // 2 - experts), jnp.bfloat16)
    probs = jnp.concatenate([high, room, low, room], axis=1)

    def place(array):
        return jnp.dot(placing, array, preferred_element_type=jnp.float32).astype(jnp.bfloat16)

    feats = jnp.stack(
        [place(tokens).reshape(flight, CAP, locals_, width),
         place(upstream).reshape(flight, CAP, locals_, width)], axis=1
    ).reshape(flight * 2 * CAP, locals_, width)
    tail = jnp.broadcast_to(
        place(probs).reshape(flight, 1, CAP, 1, PAD), (flight, 2, CAP, locals_, PAD)
    ).reshape(flight * 2 * CAP, locals_, PAD)
    send = jnp.swapaxes(jnp.concatenate([feats, tail], axis=2), 0, 1)

    rows_all, hidden_all, part, logits, home = run_exchange(send, w_in, w_out, nodes, locals_)

    pairs = [
        (n * locals_ + l, nodes * l + n) for n in range(nodes) for l in range(locals_)
    ]
    router_grad = lax.ppermute(part[:, :experts], ("node", "local"), pairs)
    w_out_grad, w_in_grad = weight_grads(rows_all, hidden_all, width)
    home_logits = logits.reshape(flight, 8, PAD)[:, :CAP, :experts].astype(jnp.bfloat16)
    router_part = contract(home_logits.reshape(flight * CAP, experts), router_weight, 1, 1)
    home_rows = jnp.swapaxes(home, 0, 1).reshape(flight * CAP, model_width)
    total = (home_rows + router_part).astype(jnp.bfloat16)
    token_grads = contract(placing, total, 0, 0).astype(jnp.bfloat16)
    return (token_grads, w_in_grad, w_out_grad, router_grad)


def solution(mesh):
    in_specs = (
        P(("node", "local"), None),
        P(("node", "local"), None),
        P(("node", "local"), None),
        P(("node", "local"), None),
        P(("node", "local"), None),
        P(None, "local", "node"),
        P(None, "node", "local"),
        P(),
    )
    out_specs = (
        P(("node", "local"), None),
        P(None, "local", "node"),
        P(None, "node", "local"),
        P(("node", "local"), None),
    )
    return jax.shard_map(local, mesh=mesh, in_specs=in_specs, out_specs=out_specs, check_vma=False)
```
